512 devices in a mesh: fsdp: 64 (over y, z), tp: 8 (over x, core).
Axes of the slice: x: 4, y: 8, z: 8, core: 2. Of those that a mesh axis runs over, the one named last changes fastest.
Arguments:
- hidden_prev: bfloat16 [12288, 2048], P('fsdp', 'tp'), may hold values from -6 to 6
- next_ids: int32 [12288], P('fsdp'), may hold values from 0 to 8191
- embed_table: bfloat16 [8192, 2048], P('fsdp', 'tp'), may hold values from -6 to 6
- embed_gain: float32 [2048], P('tp'), may hold values from 0.5 to 1.5
- hidden_gain: float32 [2048], P('tp'), may hold values from 0.5 to 1.5
- join_embed: bfloat16 [2048, 2048], P('tp', 'fsdp'), may hold values from -0.09375 to 0.09375
- join_hidden: bfloat16 [2048, 2048], P('tp', 'fsdp'), may hold values from -0.09375 to 0.09375
- final_gain: float32 [2048], replicated, may hold values from 0.5 to 1.5
- head: bfloat16 [2048, 16384], P('fsdp', 'tp'), may hold values from -7.6 to 7.6
Outputs:
- log_probs: float32 [12288, 16384], P('fsdp', 'tp')
The draws below stay inside these ranges and needn't reach their ends.
All inputs are finite; a program needn't handle non-finite values.
Results may differ from the reference program's by a relative error of at most 0.0035.
Values may be sent and summed in bfloat16 or wider, within the bound.
No kernel may reach another device: no remote copies, remote signals or barrier semaphores. Data moves between devices by JAX's collectives and lax.ppermute only.
A program may use at most 64 MiB of HBM per device.

```python
import math
import jax
import jax.numpy as jnp
import numpy as np
from jax import lax

D = 2048
GROUP = 16384
EMB = 8192
ROWS = 192
TOKENS = 12288
N_FSDP = 64


head_scale = 0.0662913


shared_scale = 50.0


def draw_head(key, part):
    key = jax.random.fold_in(key, 11)
    sign_key = jax.random.fold_in(key, 2)
    signs = jnp.where(jax.random.bernoulli(sign_key, 0.5, (D, 1)), 1.0, -1.0).astype(jnp.float32)
    feature = lax_free_iota = jnp.arange(D, dtype=jnp.int32)[:, None]
    direction = jnp.where(lax_free_iota < 64, signs * 0.125, 0.0).astype(jnp.float32)
    values = jnp.clip(jax.random.normal(key, (D, GROUP), jnp.float32), -4.0, 4.0)
    return (values * head_scale + shared_scale * direction).astype(jnp.bfloat16)


def with_ends(values, own_key, least, top_value):
    dims = values.shape
    spot = [jax.random.randint(jax.random.fold_in(own_key, axis), (), 0, dims[axis]) for axis in range(len(dims))]
    values = values.at[tuple(spot)].set(least)
    longest = dims.index(max(dims))
    spot[longest] = (spot[longest] + 1) % dims[longest]
    return values.at[tuple(spot)].set(top_value)


def block_scale(key, extent, cuts, low, high):
    level = 1.0
    for position, blocks in cuts:
        heights = jax.random.uniform(jax.random.fold_in(jax.random.fold_in(key, 6), position), (blocks,), jnp.float32, low / len(cuts), high / len(cuts))
        level = level * jnp.repeat(jnp.exp(heights), extent[position] // blocks).reshape((-1,) + (1,) * (len(extent) - 1 - position))
    return level


def rank_table(count, lean):
    weights = [(1 << 20) // math.isqrt(rank ** lean) + 1 for rank in range(1, count + 1)]
    scale = 1 + sum(weights) // (1 << 30)
    return np.cumsum(np.array([max(1, weight // scale) for weight in weights]))


def ranked_ids(stream_key, shape, amount, slope):
    grid = rank_table(amount, slope)
    lot = jax.random.randint(jax.random.fold_in(stream_key, 1), shape, 0, int(grid[amount - 1]))
    rank = jnp.searchsorted(jnp.asarray(grid, jnp.int32), lot, side="right")
    return jax.random.permutation(jax.random.fold_in(stream_key, 2), amount)[rank].astype(jnp.int32)


def centred(stream_key, extent, deviation, most, shards=(), kind=jnp.bfloat16):
    result = jax.random.normal(stream_key, extent, jnp.float32) * deviation
    if len(shards) > 0:
        result = block_scale(stream_key, extent, shards, -0.22, 0.18) * result
    return jnp.clip(result, min=-most, max=most).astype(kind)


def setup_inputs(seed: int = 0) -> dict:
    splits = jax.random.split(jax.random.key(seed), 10)
    hidden_prev = centred(splits[0], (TOKENS, D), 1.0, 6.0, ((0, 64), (1, 8)))
    next_ids = with_ends(ranked_ids(splits[1], (TOKENS,), EMB, 1), jax.random.fold_in(splits[1], 3), 0, EMB - 1).astype(jnp.int32)
    embed_table = centred(splits[2], (EMB, D), 1.0, 6.0, ((0, 64), (1, 8)))
    embed_gain = jnp.clip(1.0 + 0.1 * jax.random.normal(splits[3], (D,), jnp.float32), 0.5, 1.5)
    hidden_gain = jnp.clip(1.0 + 0.1 * jax.random.normal(splits[4], (D,), jnp.float32), 0.5, 1.5)
    join_embed = centred(splits[5], (D, D), (2 * D) ** -0.5, 0.09375, ((0, 8), (1, 64)))
    join_hidden = centred(splits[6], (D, D), (2 * D) ** -0.5, 0.09375, ((0, 8), (1, 64)))
    final_gain = jnp.clip(1.0 + 0.1 * jax.random.normal(splits[7], (D,), jnp.float32), 0.5, 1.5)
    head = draw_head(jax.random.fold_in(splits[9], 71), 0)
    return {"hidden_prev": hidden_prev, "next_ids": next_ids, "embed_table": embed_table, "embed_gain": embed_gain, "hidden_gain": hidden_gain, "join_embed": join_embed, "join_hidden": join_hidden, "final_gain": final_gain, "head": head}


eps = 1e-06

def rms_norm(values, gain):
    wide = values.astype(jnp.float32)
    mean_sq = lax.optimization_barrier(jnp.mean(wide * wide, axis=-1, keepdims=True))
    return (wide * lax.rsqrt(mean_sq + eps) * gain).astype(jnp.bfloat16)

def reference(hidden_prev, next_ids, embed_table, embed_gain, hidden_gain, join_embed, join_hidden, final_gain, head):
    embedded = jnp.take(embed_table, next_ids, axis=0)
    embed_norm = rms_norm(embedded, embed_gain)
    hidden_norm = rms_norm(hidden_prev, hidden_gain)
    joined = (jnp.dot(embed_norm, join_embed, preferred_element_type=jnp.float32) + jnp.dot(hidden_norm, join_hidden, preferred_element_type=jnp.float32)).astype(jnp.bfloat16)
    final = rms_norm(joined, final_gain)
    blocks = final.reshape(N_FSDP, ROWS, D)

    def one_block(block):
        logits = jnp.dot(block, head, preferred_element_type=jnp.float32)
        highest = lax.optimization_barrier(jnp.max(logits, axis=1, keepdims=True))
        totals = lax.optimization_barrier(jnp.sum(jnp.exp(logits - highest), axis=1, keepdims=True))
        return logits - highest - jnp.log(totals)
    return lax.map(one_block, blocks).reshape(TOKENS, GROUP)
```

```python
import jax
import jax.numpy as jnp
from jax import lax
from jax.experimental import pallas as pl
from jax.experimental.pallas import tpu as pltpu
from jax.sharding import Mesh, PartitionSpec as P

D = 2048
eps = 1e-06
FS = ("y", "z")
TP = ("x", "core")
NY, NZ, NT = 8, 8, 8
f32 = jnp.float32
bf16 = jnp.bfloat16
CONTRACT = (((1,), (1,)), ((), ()))
UP = [(i, (i + 1) % NY) for i in range(NY)]
DOWN = [(i, (i - 1) % NY) for i in range(NY)]


def scaled(values, squares, gain):
    return (values.astype(f32) * lax.rsqrt(squares / D + eps) * gain).astype(bf16)


def row_squares(values):
    wide = values.astype(f32)
    return jnp.sum(wide * wide, axis=1)


def spread(block, axes, count):
    copies = jnp.broadcast_to(block[None], (count,) + block.shape)
    return lax.all_to_all(copies, axes, 0, 0, tiled=True)


def join_kernel(found_ref, hidden_ref, *refs):
    out_ref = refs[-1]
    embed = found_ref[0].astype(f32)
    for k in range(1, found_ref.shape[0]):
        embed = embed + found_ref[k].astype(f32)
    embed = embed.astype(bf16)
    hidden = hidden_ref[...]
    width = hidden.shape[1]
    for j, ref in enumerate(refs[:-1]):
        cols = ref.shape[1] // 2
        count = ref.shape[0] * cols
        embed_proj = ref[:, :cols, :].reshape(count, width)
        hidden_proj = ref[:, cols:, :].reshape(count, width)
        total = lax.dot_general(embed, embed_proj, CONTRACT, preferred_element_type=f32)
        total += lax.dot_general(hidden, hidden_proj, CONTRACT, preferred_element_type=f32)
        out_ref[:, j * count : (j + 1) * count] = total.astype(bf16)


def join(found, hidden, blocks):
    rows = hidden.shape[0]
    return pl.pallas_call(
        join_kernel,
        out_shape=jax.ShapeDtypeStruct((rows, D), bf16),
        in_specs=[pl.BlockSpec(memory_space=pltpu.VMEM)] * (2 + len(blocks)),
        out_specs=pl.BlockSpec(memory_space=pltpu.VMEM),
        compiler_params=pltpu.CompilerParams(vmem_limit_bytes=16 * 2**20),
        cost_estimate=pl.CostEstimate(flops=4 * rows * 256 * D, bytes_accessed=4 * 2**20, transcendentals=0),
    )(found, hidden, *blocks)


def shards(hidden_prev, next_ids, embed_table, embed_gain, hidden_gain, join_embed, join_hidden, final_gain, head):
    rows = next_ids.shape[0]
    width = hidden_prev.shape[1]
    vocab = embed_table.shape[0]

    head_all = lax.all_gather(head, FS, axis=0, tiled=True)

    low = jnp.stack([next_ids // 64, next_ids % 64]).astype(bf16)
    low = jnp.pad(low, ((0, 14), (0, width - rows)))
    line = spread(jnp.concatenate([join_embed.T, join_hidden.T, low], axis=0), "z", NZ)
    part = lax.all_gather(embed_table, "y", axis=0, tiled=True)
    line, part = lax.optimization_barrier((line, part))
    cols = 2 * join_embed.shape[1]
    low = line[:, cols : cols + 2, :rows].astype(jnp.int32)
    ids = (low[:, 0] * 64 + low[:, 1]).reshape(-1)
    line = line[:, :cols]

    down, up = lax.ppermute(line, "y", DOWN), lax.ppermute(line, "y", UP)
    squares = lax.psum(jnp.concatenate([row_squares(part), row_squares(hidden_prev)]), TP)
    down, up, squares = lax.optimization_barrier((down, up, squares))
    down2, up2 = lax.ppermute(down, "y", DOWN), lax.ppermute(up, "y", UP)
    table_norm = scaled(part, squares[: NY * vocab, None], embed_gain)
    hidden_norm = scaled(hidden_prev, squares[NY * vocab :, None], hidden_gain)
    row = lax.iota(jnp.int32, NY * vocab)
    place = (row // vocab * NZ + lax.axis_index("z")) * vocab + row % vocab
    one_hot = (ids[:, None] == place[None, :]).astype(bf16)
    found = jnp.dot(one_hot, table_norm, preferred_element_type=f32).astype(bf16)
    found = lax.all_to_all(found.reshape(NZ, rows, width), "z", 0, 0, tiled=True)
    down3, up3 = lax.ppermute(down2, "y", DOWN), lax.ppermute(up2, "y", UP)
    up4 = lax.ppermute(up3, "y", UP)
    blocks = [line, down, down2, down3, up4, up3, up2, up]

    share = join(found, hidden_norm, blocks)
    shares = lax.all_to_all(share.reshape(NT, rows // NT, D), TP, 0, 0, tiled=True)
    joined = jnp.sum(shares.astype(f32), axis=0).astype(bf16)
    twice = jnp.concatenate([joined, joined], axis=1)
    joined = lax.dynamic_slice_in_dim(twice, (NY - lax.axis_index("y")) % NY * (D // NY), D, axis=1)
    final_part = scaled(joined, row_squares(joined)[:, None], final_gain)
    final = lax.all_gather(final_part, TP, axis=0, tiled=True)

    logits = jnp.dot(final, head_all, preferred_element_type=f32)
    local_max = jnp.max(logits, axis=1)
    local_sum = jnp.sum(jnp.exp(logits - local_max[:, None]), axis=1)
    both = spread(jnp.stack([local_max, local_sum]), TP, NT)
    highest = jnp.max(both[:, 0], axis=0)
    total = jnp.sum(both[:, 1] * jnp.exp(both[:, 0] - highest), axis=0)
    return logits - highest[:, None] - jnp.log(total)[:, None]


def solution(mesh):
    mesh = Mesh(mesh.devices.reshape(NY, NZ, NT // 2, 2), FS + TP)
    return jax.shard_map(
        shards,
        mesh=mesh,
        in_specs=(
            P(FS, TP),
            P(FS),
            P(FS, TP),
            P(TP),
            P(TP),
            P(TP, FS),
            P(TP, FS),
            P(),
            P(FS, TP),
        ),
        out_specs=P(FS, TP),
        check_vma=False,
    )
```

```python
import jax
import jax.numpy as jnp
from jax import lax
from jax.experimental import pallas as pl
from jax.experimental.pallas import tpu as pltpu
from jax.sharding import Mesh, PartitionSpec as P

D = 2048
eps = 1e-06
FS = ("y", "z")
TP = ("x", "core")
NY, NZ, NT = 8, 8, 8
f32 = jnp.float32
bf16 = jnp.bfloat16
CONTRACT = (((1,), (1,)), ((), ()))
UP = [(i, (i + 1) % NY) for i in range(NY)]
ACROSS = [(i, (i + NY // 2) % NY) for i in range(NY)]
DOWN = [(i, (i - 1) % NY) for i in range(NY)]


def row_squares(values):
    wide = values.astype(f32)
    return jnp.sum(wide * wide, axis=1)


def spread(block, axes, count):
    copies = jnp.broadcast_to(block[None], (count,) + block.shape)
    return lax.all_to_all(copies, axes, 0, 0, tiled=True)


def join_kernel(embed_ref, hidden_ref, embed_scale_ref, hidden_scale_ref, *refs):
    out_ref = refs[-1]
    embed, hidden = embed_ref[...], hidden_ref[...]
    embed_scale, hidden_scale = embed_scale_ref[...], hidden_scale_ref[...]
    width = hidden.shape[1]
    for j, ref in enumerate(refs[:-1]):
        cols = ref.shape[1] // 2
        count = ref.shape[0] * cols
        embed_proj = ref[:, :cols, :].reshape(count, width)
        hidden_proj = ref[:, cols:, :].reshape(count, width)
        total = embed_scale * lax.dot_general(embed, embed_proj, CONTRACT, preferred_element_type=f32)
        total += hidden_scale * lax.dot_general(hidden, hidden_proj, CONTRACT, preferred_element_type=f32)
        out_ref[:, j * count : (j + 1) * count] = total.astype(bf16)


def join(embed, hidden, embed_scale, hidden_scale, blocks):
    rows = hidden.shape[0]
    return pl.pallas_call(
        join_kernel,
        out_shape=jax.ShapeDtypeStruct((rows, D), bf16),
        in_specs=[pl.BlockSpec(memory_space=pltpu.VMEM)] * (4 + len(blocks)),
        out_specs=pl.BlockSpec(memory_space=pltpu.VMEM),
        compiler_params=pltpu.CompilerParams(vmem_limit_bytes=16 * 2**20),
        cost_estimate=pl.CostEstimate(flops=4 * rows * 256 * D, bytes_accessed=4 * 2**20, transcendentals=0),
    )(embed, hidden, embed_scale, hidden_scale, *blocks)


def shards(hidden_prev, next_ids, embed_table, embed_gain, hidden_gain, join_embed, join_hidden, final_gain, head):
    rows = next_ids.shape[0]
    width = hidden_prev.shape[1]
    vocab = embed_table.shape[0]
    cols = 2 * join_embed.shape[1]

    head_all = lax.all_gather(head, FS, axis=0, tiled=True)

    next_ids = next_ids.reshape(NT // 2, 2, rows // NT).swapaxes(0, 1).reshape(rows)
    hidden_prev = hidden_prev.reshape(NT // 2, 2, rows // NT, width).swapaxes(0, 1).reshape(rows, width)

    part = spread(embed_table, "y", NY).reshape(NY * vocab, width)
    low = jnp.stack([next_ids // 64, next_ids % 64]).astype(bf16)
    low = jnp.pad(low, ((0, 14), (0, width - rows)))
    own = jnp.concatenate([join_embed.T, join_hidden.T], axis=0)
    far = lax.ppermute(own, "y", ACROSS)
    line = lax.all_gather(jnp.concatenate([own, far, low], axis=0), "z", axis=0)
    line, part = lax.optimization_barrier((line, part))
    low = line[:, 2 * cols : 2 * cols + 2, :rows].astype(jnp.int32)
    ids = (low[:, 0] * 64 + low[:, 1]).reshape(-1)
    far, line = line[:, cols : 2 * cols], line[:, :cols]

    down, up = lax.ppermute(line, "y", DOWN), lax.ppermute(line, "y", UP)
    row = lax.iota(jnp.int32, NY * vocab)
    place = (row // vocab * NZ + lax.axis_index("z")) * vocab + row % vocab
    one_hot = (ids[:, None] == place[None, :]).astype(bf16)
    found = jnp.dot(one_hot, part, preferred_element_type=f32).astype(bf16)
    found = lax.all_to_all(found.reshape(NZ, rows, width), "z", 0, 0, tiled=True)
    down2, up2 = lax.ppermute(down, "y", DOWN), lax.ppermute(up, "y", UP)
    down3, up3 = lax.ppermute(far, "y", DOWN), lax.ppermute(far, "y", UP)
    blocks = [line, down, down2, up3, far, down3, up2, up]

    embedded = jnp.sum(found.astype(f32), axis=0)
    squares = jnp.stack([row_squares(embedded), row_squares(hidden_prev)])
    squares = lax.psum(squares, TP)
    scales = lax.rsqrt(squares / D + eps)[:, :, None]
    embedded = (embedded * embed_gain).astype(bf16)
    hidden = (hidden_prev.astype(f32) * hidden_gain).astype(bf16)
    share = join(embedded, hidden, scales[0], scales[1], blocks)
    pair = lax.all_to_all(share.reshape(2, rows // 2, D), "core", 0, 0, tiled=True)
    share = jnp.sum(pair.astype(f32), axis=0).astype(bf16)
    shares = lax.all_to_all(share.reshape(NT // 2, rows // NT, D), "x", 0, 0, tiled=True)
    joined = jnp.sum(shares.astype(f32), axis=0).astype(bf16)
    twice = jnp.concatenate([joined, joined], axis=1)
    joined = lax.dynamic_slice_in_dim(twice, (NY - lax.axis_index("y")) % NY * (D // NY), D, axis=1)
    wide = joined.astype(f32)
    final_part = (wide * lax.rsqrt(row_squares(joined)[:, None] / D + eps) * final_gain).astype(bf16)
    final = lax.all_gather(final_part, TP, axis=0, tiled=True)

    logits = jnp.dot(final, head_all, preferred_element_type=f32)
    local_max = jnp.max(logits, axis=1)
    local_sum = jnp.sum(jnp.exp(logits - local_max[:, None]), axis=1)
    both = spread(jnp.stack([local_max, local_sum]), TP, NT)
    highest = jnp.max(both[:, 0], axis=0)
    total = jnp.sum(both[:, 1] * jnp.exp(both[:, 0] - highest), axis=0)
    return logits - highest[:, None] - jnp.log(total)[:, None]


def solution(mesh):
    mesh = Mesh(mesh.devices.reshape(NY, NZ, NT // 2, 2), FS + TP)
    return jax.shard_map(
        shards,
        mesh=mesh,
        in_specs=(
            P(FS, TP),
            P(FS),
            P(FS, TP),
            P(TP),
            P(TP),
            P(TP, FS),
            P(TP, FS),
            P(),
            P(FS, TP),
        ),
        out_specs=P(FS, TP),
        check_vma=False,
    )
```

```python
import jax
import jax.numpy as jnp
from jax import lax
from jax.experimental import pallas as pl
from jax.experimental.pallas import tpu as pltpu
from jax.sharding import Mesh, PartitionSpec as P

D = 2048
eps = 1e-06
FS = ("y", "z")
TP = ("x", "core")
NY, NZ, NT = 8, 8, 8
f32 = jnp.float32
bf16 = jnp.bfloat16
CONTRACT = (((1,), (1,)), ((), ()))
UP = [(i, (i + 1) % NY) for i in range(NY)]
ACROSS = [(i, (i + NY // 2) % NY) for i in range(NY)]
DOWN = [(i, (i - 1) % NY) for i in range(NY)]


def row_squares(values):
    wide = values.astype(f32)
    return jnp.sum(wide * wide, axis=1)


def spread(block, axes, count):
    copies = jnp.broadcast_to(block[None], (count,) + block.shape)
    return lax.all_to_all(copies, axes, 0, 0, tiled=True)


def join_kernel(embed_ref, hidden_ref, embed_scale_ref, hidden_scale_ref, *refs):
    out_ref = refs[-1]
    embed, hidden = embed_ref[...], hidden_ref[...]
    embed_scale, hidden_scale = embed_scale_ref[...], hidden_scale_ref[...]
    width = hidden.shape[1]
    for j, ref in enumerate(refs[:-1]):
        cols = ref.shape[1] // 2
        count = ref.shape[0] * cols
        embed_proj = ref[:, :cols, :].reshape(count, width)
        hidden_proj = ref[:, cols:, :].reshape(count, width)
        total = embed_scale * lax.dot_general(embed, embed_proj, CONTRACT, preferred_element_type=f32)
        total += hidden_scale * lax.dot_general(hidden, hidden_proj, CONTRACT, preferred_element_type=f32)
        out_ref[:, j * count : (j + 1) * count] = total.astype(bf16)


def join(embed, hidden, embed_scale, hidden_scale, blocks):
    rows = hidden.shape[0]
    return pl.pallas_call(
        join_kernel,
        out_shape=jax.ShapeDtypeStruct((rows, D), bf16),
        in_specs=[pl.BlockSpec(memory_space=pltpu.VMEM)] * (4 + len(blocks)),
        out_specs=pl.BlockSpec(memory_space=pltpu.VMEM),
        compiler_params=pltpu.CompilerParams(vmem_limit_bytes=16 * 2**20),
        cost_estimate=pl.CostEstimate(flops=4 * rows * 256 * D, bytes_accessed=4 * 2**20, transcendentals=0),
    )(embed, hidden, embed_scale, hidden_scale, *blocks)


def shards(hidden_prev, next_ids, embed_table, embed_gain, hidden_gain, join_embed, join_hidden, final_gain, head):
    rows = next_ids.shape[0]
    width = hidden_prev.shape[1]
    vocab = embed_table.shape[0]
    cols = 2 * join_embed.shape[1]

    head_all = lax.all_gather(head, FS, axis=0, tiled=True)

    next_ids = next_ids.reshape(NT // 2, 2, rows // NT).swapaxes(0, 1).reshape(rows)
    hidden_prev = hidden_prev.reshape(NT // 2, 2, rows // NT, width).swapaxes(0, 1).reshape(rows, width)

    part = spread(embed_table, "y", NY).reshape(NY * vocab, width)
    low = jnp.stack([next_ids // 64, next_ids % 64]).astype(bf16)
    low = jnp.pad(low, ((0, 14), (0, width - rows)))
    own = jnp.concatenate([join_embed.T, join_hidden.T], axis=0)
    far = lax.ppermute(own, "y", ACROSS)
    line = lax.all_gather(jnp.concatenate([own, far, low], axis=0), "z", axis=0)
    line, part = lax.optimization_barrier((line, part))
    low = line[:, 2 * cols : 2 * cols + 2, :rows].astype(jnp.int32)
    ids = (low[:, 0] * 64 + low[:, 1]).reshape(-1)
    far, line = line[:, cols : 2 * cols], line[:, :cols]

    down, up = lax.ppermute(line, "y", DOWN), lax.ppermute(line, "y", UP)
    row = lax.iota(jnp.int32, NY * vocab)
    place = (row // vocab * NZ + lax.axis_index("z")) * vocab + row % vocab
    one_hot = (ids[:, None] == place[None, :]).astype(bf16)
    found = jnp.dot(one_hot, part, preferred_element_type=f32).astype(bf16)
    found = lax.all_to_all(found.reshape(NZ, rows, width), "z", 0, 0, tiled=True)
    down2, up2 = lax.ppermute(down, "y", DOWN), lax.ppermute(up, "y", UP)
    down3, up3 = lax.ppermute(far, "y", DOWN), lax.ppermute(far, "y", UP)
    blocks = [line, down, down2, up3, far, down3, up2, up]

    embedded = jnp.sum(found.astype(f32), axis=0)
    squares = jnp.stack([row_squares(embedded), row_squares(hidden_prev)])
    squares = lax.psum(lax.optimization_barrier(lax.psum(squares, "core")), "x")
    scales = lax.rsqrt(squares / D + eps)[:, :, None]
    embedded = (embedded * embed_gain).astype(bf16)
    hidden = (hidden_prev.astype(f32) * hidden_gain).astype(bf16)
    share = join(embedded, hidden, scales[0], scales[1], blocks)
    pair = lax.all_to_all(share.reshape(2, rows // 2, D), "core", 0, 0, tiled=True)
    share = jnp.sum(pair.astype(f32), axis=0).astype(bf16)
    shares = lax.all_to_all(share.reshape(NT // 2, rows // NT, D), "x", 0, 0, tiled=True)
    joined = jnp.sum(shares.astype(f32), axis=0).astype(bf16)
    twice = jnp.concatenate([joined, joined], axis=1)
    joined = lax.dynamic_slice_in_dim(twice, (NY - lax.axis_index("y")) % NY * (D // NY), D, axis=1)
    wide = joined.astype(f32)
    final_part = (wide * lax.rsqrt(row_squares(joined)[:, None] / D + eps) * final_gain).astype(bf16)
    final = lax.all_gather(final_part, TP, axis=0, tiled=True)

    logits = jnp.dot(final, head_all, preferred_element_type=f32)
    local_max = jnp.max(logits, axis=1)
    local_sum = jnp.sum(jnp.exp(logits - local_max[:, None]), axis=1)
    both = spread(jnp.stack([local_max, local_sum]), TP, NT)
    highest = jnp.max(both[:, 0], axis=0)
    total = jnp.sum(both[:, 1] * jnp.exp(both[:, 0] - highest), axis=0)
    return logits - highest[:, None] - jnp.log(total)[:, None]


def solution(mesh):
    mesh = Mesh(mesh.devices.reshape(NY, NZ, NT // 2, 2), FS + TP)
    return jax.shard_map(
        shards,
        mesh=mesh,
        in_specs=(
            P(FS, TP),
            P(FS),
            P(FS, TP),
            P(TP),
            P(TP),
            P(TP, FS),
            P(TP, FS),
            P(),
            P(FS, TP),
        ),
        out_specs=P(FS, TP),
        check_vma=False,
    )
```
